128 devices in a mesh: dp: 4 (over z), head: 32 (over y, x, core).
Axes of the slice: x: 4, y: 4, z: 4, core: 2. Of those that a mesh axis runs over, the one named last changes fastest.
Arguments:
- queries: bfloat16 [24576, 4096], P(('dp', 'head')), parts along dimension 0, may hold values from -6 to 6
- key_vectors: bfloat16 [24576, 4096], P(('dp', 'head')), parts along dimension 0, may hold values from -6 to 6
- values: bfloat16 [24576, 4096], P(('dp', 'head')), parts along dimension 0, may hold values from -6 to 6
- out_grad: bfloat16 [24576, 4096], P(('dp', 'head')), parts along dimension 0, may hold values from -6 to 6
- output: bfloat16 [24576, 4096], P(('dp', 'head')), parts along dimension 0, may hold values from -3 to 3
- key_blocks: int32 [128, 48, 12], P(('dp', 'head')), parts along dimension 0, may hold values from 0 to 47, as said below
- block_count: int32 [128, 48], P(('dp', 'head')), parts along dimension 0, may hold values from 2 to 12, as said below
Outputs:
- query_grad: bfloat16 [24576, 4096], P(('dp', 'head')), parts along dimension 0
- key_grad: bfloat16 [24576, 4096], P(('dp', 'head')), parts along dimension 0
- value_grad: bfloat16 [24576, 4096], P(('dp', 'head')), parts along dimension 0
The draws below stay inside these ranges and needn't reach their ends.
There are 4 independent parts, one for each index of `dp`. The reference program is written for one: setup_inputs(seed, part) draws one part's arguments, and reference() takes and returns one part's arrays. A program takes and returns all parts, laid end to end along the dimension named above; each array names one. Nothing has to cross between parts.
Inputs may be any that keep to these rules, and one draw needn't show every extreme that they name: `key_blocks`: slot 0 of every query block names the block itself; the live slots of one query block name different blocks; slots at or past block_count hold block numbers that are ignored. `block_count`: every head has a query block with exactly 12 live slots.
All inputs are finite; a program needn't handle non-finite values.
Results may differ from the reference program's by a relative error of at most 0.0049.
Values may be sent and summed in bfloat16 or wider, within the bound.
No kernel may reach another device: no remote copies, remote signals or barrier semaphores. Data moves between devices by JAX's collectives and lax.ppermute only.
A program may use at most 128 MiB of HBM per device.

```python
import jax
import jax.numpy as jnp
from jax import lax

HD = 128
HEADS = 32
TOKENS = 6144
BLK = 128
KMAX = 12


def draw_queries(key, part):
    key = jax.random.fold_in(key, 11)
    base = jnp.clip(jax.random.normal(key, (TOKENS, HEADS * HD), jnp.float32), -6.0, 6.0)
    return base.astype(jnp.bfloat16)


def draw_key_vectors(key, part):
    key = jax.random.fold_in(key, 23)
    base = jnp.clip(jax.random.normal(key, (TOKENS, HEADS * HD), jnp.float32), -6.0, 6.0)
    return base.astype(jnp.bfloat16)


def draw_key_blocks(key, part):
    key = jax.random.fold_in(key, 37)
    blocks_total = TOKENS // BLK
    raw = jax.random.randint(key, (HEADS, blocks_total, blocks_total - 1), 0, 1 << 16)
    scores = raw * blocks_total + jnp.arange(blocks_total - 1, dtype=jnp.int32)[None, None, :]
    order = jnp.argsort(scores, axis=-1).astype(jnp.int32)
    offsets = order[:, :, :KMAX - 1] + 1
    own_block = jnp.arange(blocks_total, dtype=jnp.int32)[None, :, None]
    others = (own_block + offsets) % blocks_total
    own_full = jnp.broadcast_to(own_block, (HEADS, blocks_total, 1))
    return jnp.concatenate([own_full, others], axis=-1).astype(jnp.int32)


def draw_block_count(key, part):
    key = jax.random.fold_in(key, 53)
    blocks_total = TOKENS // BLK
    heavy = jax.random.randint(jax.random.fold_in(key, 1), (HEADS, 1), 4, KMAX + 1)
    raw = jax.random.randint(jax.random.fold_in(key, 2), (HEADS, blocks_total), 0, 1 << 20)
    counts = 2 + raw % (heavy - 1)
    position = jax.random.randint(jax.random.fold_in(key, 3), (HEADS, 1), 0, blocks_total)
    columns = jnp.arange(blocks_total, dtype=jnp.int32)[None, :]
    return jnp.where(columns == position, KMAX, counts).astype(jnp.int32)


def block_scale(key, dims, split, least, top_value):
    factor_of = 1.0
    for dim, shards_of in split:
        steps = jax.random.uniform(jax.random.fold_in(jax.random.fold_in(key, 6), dim), (shards_of,), jnp.float32, least / len(split), top_value / len(split))
        factor_of = factor_of * jnp.repeat(jnp.exp(steps), dims[dim] // shards_of).reshape((-1,) + (1,) * (len(dims) - 1 - dim))
    return factor_of


def noise(stream_key, dims, scale, most, cuts=(), held_as=jnp.bfloat16):
    drawn = scale * jax.random.normal(stream_key, dims, jnp.float32)
    if cuts:
        drawn = drawn * block_scale(stream_key, dims, cuts, -0.22, 0.18)
    return jnp.clip(drawn, -most, most).astype(held_as)


def setup_inputs(seed: int = 0, part: int = 0) -> dict:
    key_of = jax.random.split(jax.random.key(seed), 8)
    part_splits = jax.random.split(jax.random.fold_in(key_of[7], part), 8)
    queries = draw_queries(jax.random.fold_in(jax.random.fold_in(key_of[7], part), 71), part)
    key_vectors = draw_key_vectors(jax.random.fold_in(jax.random.fold_in(key_of[7], part), 71), part)
    values = noise(part_splits[2], (TOKENS, HEADS * HD), 1.0, 6.0, ((0, 32),))
    out_grad = noise(part_splits[3], (TOKENS, HEADS * HD), 1.0, 6.0, ((0, 32),))
    output = noise(part_splits[4], (TOKENS, HEADS * HD), 0.3, 3.0, ((0, 32),))
    key_blocks = draw_key_blocks(jax.random.fold_in(jax.random.fold_in(key_of[7], part), 71), part)
    block_count = draw_block_count(jax.random.fold_in(jax.random.fold_in(key_of[7], part), 71), part)
    return {"queries": queries, "key_vectors": key_vectors, "values": values, "out_grad": out_grad, "output": output, "key_blocks": key_blocks, "block_count": block_count}


def pick_group(blocks_total):
    for size_try in (8, 4, 2, 1):
        if blocks_total % size_try == 0:
            return size_try
    return 1


def head_gradients(queries, key_vectors, values, out_grad, row_terms, key_blocks, block_count):
    blocks_total = queries.shape[0] // BLK
    group = pick_group(blocks_total)
    steps_total = blocks_total // group
    scale_factor = HD ** -0.5
    key_tiles = key_vectors.astype(jnp.float32).reshape(blocks_total, BLK, HD)
    value_tiles = values.astype(jnp.float32).reshape(blocks_total, BLK, HD)
    stacked = (queries.astype(jnp.float32).reshape(steps_total, group, BLK, HD),
               out_grad.astype(jnp.float32).reshape(steps_total, group, BLK, HD),
               row_terms.reshape(steps_total, group, BLK),
               key_blocks.astype(jnp.int32).reshape(steps_total, group, KMAX),
               block_count.astype(jnp.int32).reshape(steps_total, group))

    def one_step(carry, items):
        key_acc, value_acc = carry
        query_tile, grad_tile, term_tile, index_tile, count_tile = items
        chosen_keys = key_tiles[index_tile]
        chosen_values = value_tiles[index_tile]
        scores = jnp.einsum('gqd,gkjd->gqkj', query_tile, chosen_keys) * scale_factor
        slot_ids = jnp.arange(KMAX, dtype=jnp.int32)
        live = slot_ids[None, :] < count_tile[:, None]
        scores = jnp.where(live[:, None, :, None], scores, -1e30)
        top = jnp.max(scores, axis=(2, 3), keepdims=True)
        weights = jnp.exp(scores - top)
        probs = weights / jnp.sum(weights, axis=(2, 3), keepdims=True)
        probs_low = lax.optimization_barrier(probs.astype(jnp.bfloat16)).astype(jnp.float32)
        value_part = jnp.einsum('gqkj,gqd->gkjd', probs_low, grad_tile)
        prob_grad = jnp.einsum('gqd,gkjd->gqkj', grad_tile, chosen_values)
        score_low = (probs * (prob_grad - term_tile[:, :, None, None])).astype(jnp.bfloat16)
        score_grad = lax.optimization_barrier(score_low).astype(jnp.float32)
        query_part = jnp.einsum('gqkj,gkjd->gqd', score_grad, chosen_keys) * scale_factor
        key_part = jnp.einsum('gqkj,gqd->gkjd', score_grad, query_tile) * scale_factor
        flat_index = index_tile.reshape(-1)
        key_acc = key_acc.at[flat_index].add(key_part.reshape(-1, BLK, HD))
        value_acc = value_acc.at[flat_index].add(value_part.reshape(-1, BLK, HD))
        return (key_acc, value_acc), query_part.astype(jnp.bfloat16)

    start_acc = jnp.zeros((blocks_total, BLK, HD), jnp.float32)
    (key_acc, value_acc), query_parts = lax.scan(one_step, (start_acc, start_acc), stacked)
    total_rows = blocks_total * BLK
    return (query_parts.reshape(total_rows, HD),
            key_acc.reshape(total_rows, HD).astype(jnp.bfloat16),
            value_acc.reshape(total_rows, HD).astype(jnp.bfloat16))


def reference(queries, key_vectors, values, out_grad, output, key_blocks, block_count):
    row_terms = jnp.sum((out_grad.astype(jnp.float32) * output.astype(jnp.float32)).reshape(TOKENS, HEADS, HD), axis=-1)

    def split_heads(array_in):
        return array_in.reshape(TOKENS, HEADS, HD).transpose(1, 0, 2)

    def per_head(items):
        return head_gradients(*items)

    results = lax.map(per_head, (split_heads(queries), split_heads(key_vectors), split_heads(values),
                                 split_heads(out_grad), row_terms.T, key_blocks, block_count))

    def join_heads(array_in):
        return array_in.transpose(1, 0, 2).reshape(TOKENS, HEADS * HD)

    return (join_heads(results[0]), join_heads(results[1]), join_heads(results[2]))
```

```python
import functools

import jax
import jax.numpy as jnp
from jax import lax
from jax.experimental import pallas as pl
from jax.experimental.pallas import tpu as pltpu
from jax.sharding import PartitionSpec as P

HD = 128
BLK = 128
SHARDS = 32
ROWS = 192
TOKENS = SHARDS * ROWS
NB = TOKENS // BLK
KMAX = 12
MAXPAIR = KMAX // 2
COLS = 4
SCALE = HD**-0.5
EXP2_SCALE = SCALE * 1.4426950408889634
NEG = -1e30
f32 = jnp.float32
bf16 = jnp.bfloat16

VMEM_SPEC = pl.BlockSpec(memory_space=pltpu.VMEM)
SMEM_SPEC = pl.BlockSpec(memory_space=pltpu.SMEM)


def dot(a, b):
    return lax.dot_general(a, b, (((1,), (0,)), ((), ())), preferred_element_type=f32)


def rows(ref, i):
    return ref[pl.ds(pl.multiple_of(i * BLK, BLK), BLK), :]


def wide(a, b):
    return jnp.concatenate([a, b], axis=1)


def diagonal(ref, x):
    ref[0:BLK, 0:BLK] = x
    ref[BLK : 2 * BLK, BLK : 2 * BLK] = x


def pack_kernel(q_ref, k_ref, g_ref, x_ref):
    for c in range(COLS):
        for i, ref in enumerate((q_ref, k_ref, g_ref)):
            x_ref[c, i] = ref[:, c * HD : (c + 1) * HD]


def pack(q, k, g):
    block = pl.BlockSpec((ROWS, COLS * HD), lambda h: (0, h))
    return pl.pallas_call(
        pack_kernel,
        grid=(SHARDS // COLS,),
        in_specs=[block] * 3,
        out_specs=pl.BlockSpec((COLS, 3, ROWS, HD), lambda h: (h, 0, 0, 0)),
        out_shape=jax.ShapeDtypeStruct((SHARDS, 3, ROWS, HD), bf16),
        cost_estimate=pl.CostEstimate(flops=0, bytes_accessed=9437184, transcendentals=0),
        name="pack_qkg",
    )(q, k, g)


def pack_values_kernel(parity_ref, v_ref, g_ref, o_ref, x_ref):
    odd = parity_ref[0] == 1
    gap = jnp.zeros((64, HD), f32)
    ones = jnp.ones((8, HD), bf16)
    sub = lax.broadcasted_iota(jnp.int32, (8, HD), 0)
    contract = (((1,), (1,)), ((), ()))
    for c in range(COLS):
        cols = slice(c * HD, (c + 1) * HD)
        x_ref[c, 0:ROWS] = v_ref[:, cols]
        prod = g_ref[:, cols].astype(f32) * o_ref[:, cols].astype(f32)
        prod = jnp.where(
            odd, jnp.concatenate([gap, prod], axis=0), jnp.concatenate([prod, gap], axis=0)
        )
        high = prod.astype(bf16)
        low = (prod - high.astype(f32)).astype(bf16)
        terms = lax.dot_general(ones, high, contract, preferred_element_type=f32)
        terms += lax.dot_general(ones, low, contract, preferred_element_type=f32)
        out = jnp.zeros((8, HD), f32)
        rest = terms
        for part in range(3):
            piece = rest.astype(bf16).astype(f32)
            rest = rest - piece
            out = jnp.where(sub == 2 * part, piece[:, :HD], out)
            out = jnp.where(sub == 2 * part + 1, piece[:, HD:], out)
        x_ref[c, ROWS : ROWS + 8] = out.astype(bf16)


def pack_values(parity, v, g, o):
    block = pl.BlockSpec((ROWS, COLS * HD), lambda h: (0, h))
    return pl.pallas_call(
        pack_values_kernel,
        grid=(SHARDS // COLS,),
        in_specs=[SMEM_SPEC] + [block] * 3,
        out_specs=pl.BlockSpec((COLS, ROWS + 8, HD), lambda h: (h, 0, 0)),
        out_shape=jax.ShapeDtypeStruct((SHARDS, ROWS + 8, HD), bf16),
        cost_estimate=pl.CostEstimate(flops=0, bytes_accessed=6291456, transcendentals=0),
        name="pack_v",
    )(parity, v, g, o)


def unpack_kernel(*refs):
    x_ref, outs = refs[0], refs[1:]
    for c in range(COLS):
        for i, ref in enumerate(outs):
            ref[:, c * HD : (c + 1) * HD] = x_ref[c, i]


def unpack(x):
    count = x.shape[1]
    return pl.pallas_call(
        unpack_kernel,
        grid=(SHARDS // COLS,),
        in_specs=[pl.BlockSpec((COLS, count, ROWS, HD), lambda h: (h, 0, 0, 0))],
        out_specs=[pl.BlockSpec((ROWS, COLS * HD), lambda h: (0, h))] * count,
        out_shape=[jax.ShapeDtypeStruct((ROWS, SHARDS * HD), bf16)] * count,
        cost_estimate=pl.CostEstimate(
            flops=0, bytes_accessed=count * 3145728, transcendentals=0
        ),
        compiler_params=pltpu.CompilerParams(vmem_limit_bytes=16 << 20),
        name="unpack",
    )(x)


def store_block(ref, part, block, value):
    for half in range(2):
        piece = 2 * block + half
        shard = piece // 3
        start = pl.multiple_of((piece - 3 * shard) * 64, 64)
        ref[shard, part, pl.ds(start, 64), :] = value[64 * half : 64 * half + 64]


def slot_pair(blocks, a, p, last, full):
    i0 = blocks[a, 2 * p]
    i1 = blocks[a, 2 * p + 1]
    if not last:
        return i0, i1, i1
    return i0, jnp.where(full, i1, i0), jnp.where(full, i1, NB)


def dead_half(full):
    lane = lax.broadcasted_iota(jnp.int32, (1, 2 * BLK), 1)
    return jnp.logical_and(lane >= BLK, jnp.logical_not(full))


def first_kernel(blocks, counts, q_ref, k_ref, g_ref, dv_ref, lse_ref, acc, st, wq, wg):
    q = q_ref.reshape(TOKENS, HD)
    k = k_ref.reshape(TOKENS, HD)
    g = g_ref.reshape(TOKENS, HD)
    acc[...] = jnp.zeros_like(acc)
    wq[...] = jnp.zeros_like(wq)
    wg[...] = jnp.zeros_like(wg)

    def work(a, n, pairs):
        full = n == 2 * pairs
        top = None
        ids = []
        for p in range(pairs):
            last = p == pairs - 1
            i0, i1, j1 = slot_pair(blocks, a, p, last, full)
            ids.append((i0, j1))
            s = dot(wide(rows(k, i0), rows(k, i1)), wq[...])
            if last:
                s = jnp.where(dead_half(full), NEG, s)
            st[p] = s
            here = jnp.max(s, axis=0, keepdims=True)
            top = here if top is None else jnp.maximum(top, here)
        top = jnp.maximum(top[:, :BLK], top[:, BLK:]) * EXP2_SCALE
        top2 = wide(top, top)
        total = None
        for p in range(pairs):
            e = jnp.exp2(st[p] * EXP2_SCALE - top2)
            st[p] = e
            here = jnp.sum(e, axis=0, keepdims=True)
            total = here if total is None else total + here
        total = total[:, :BLK] + total[:, BLK:]
        lse_ref[a] = top + jnp.log2(total)
        inverse = 1.0 / total
        inverse2 = wide(inverse, inverse)
        for p in range(pairs):
            dv = dot((st[p] * inverse2).astype(bf16), wg[...])
            i0, j1 = ids[p]
            b0 = acc[i0] + dv[:, :BLK]
            b1 = acc[j1] + dv[:, BLK:]
            acc[i0] = b0
            acc[j1] = b1

    def body(a, carry):
        n = counts[0, a]
        diagonal(wq, rows(q, a).T)
        diagonal(wg, rows(g, a))
        for pairs in range(1, MAXPAIR + 1):
            pl.when((n + 1) // 2 == pairs)(functools.partial(work, a, n, pairs))
        return carry

    lax.fori_loop(0, NB, body, 0)

    def finish(b, carry):
        store_block(dv_ref, 0, b, acc[b].astype(bf16))
        return carry

    lax.fori_loop(0, NB, finish, 0)


def second_kernel(
    blocks, counts, q_ref, k_ref, g_ref, v_ref, t_ref, lse_ref, out_ref, acc, kt, terms, wq, wg, wn
):
    q = q_ref.reshape(TOKENS, HD)
    k = k_ref.reshape(TOKENS, HD)
    g = g_ref.reshape(TOKENS, HD)
    v = v_ref.reshape(TOKENS, HD)
    acc[...] = jnp.zeros_like(acc)
    wq[...] = jnp.zeros_like(wq)
    wg[...] = jnp.zeros_like(wg)
    wn[...] = jnp.zeros_like(wn)

    def prepare(t, carry):
        a = t_ref[2 * t].astype(f32)
        b = t_ref[2 * t + 1].astype(f32)
        a0 = a[0:1] + a[2:3] + a[4:5]
        a1 = a[1:2] + a[3:4] + a[5:6]
        b0 = b[0:1] + b[2:3] + b[4:5]
        b1 = b[1:2] + b[3:4] + b[5:6]
        terms[3 * t] = a0
        terms[3 * t + 1] = a1 + b0
        terms[3 * t + 2] = b1
        for r in range(3):
            kt[3 * t + r] = rows(k, 3 * t + r).T
        return carry

    lax.fori_loop(0, NB // 3, prepare, 0)

    def work(a, n, pairs):
        full = n == 2 * pairs
        lse = wide(lse_ref[a], lse_ref[a])
        term = wide(terms[a], terms[a])
        dq = None
        for p in range(pairs):
            last = p == pairs - 1
            i0, i1, j1 = slot_pair(blocks, a, p, last, full)
            s = dot(wide(rows(k, i0), rows(k, i1)), wq[...])
            dp = dot(wide(rows(v, i0), rows(v, i1)), wg[...])
            ds = jnp.exp2(s * EXP2_SCALE - lse) * (dp - term)
            if last:
                ds = jnp.where(dead_half(full), 0.0, ds)
            ds = ds.astype(bf16)
            dk = dot(ds, wn[...])
            b0 = acc[i0] + dk[:, :BLK]
            b1 = acc[j1] + dk[:, BLK:]
            acc[i0] = b0
            acc[j1] = b1
            part = dot(
                wide(kt[i0], kt[i1]), jnp.concatenate([ds[:, :BLK], ds[:, BLK:]], axis=0)
            )
            dq = part if dq is None else dq + part
        store_block(out_ref, 0, a, (dq.T * SCALE).astype(bf16))

    def body(a, carry):
        n = counts[0, a]
        qb = rows(q, a)
        diagonal(wq, qb.T)
        diagonal(wn, qb)
        diagonal(wg, rows(g, a).T)
        for pairs in range(1, MAXPAIR + 1):
            pl.when((n + 1) // 2 == pairs)(functools.partial(work, a, n, pairs))
        return carry

    lax.fori_loop(0, NB, body, 0)

    def finish(b, carry):
        store_block(out_ref, 1, b, (acc[b] * SCALE).astype(bf16))
        return carry

    lax.fori_loop(0, NB, finish, 0)


def part_specs(count):
    return [
        pl.BlockSpec((SHARDS, None, ROWS, HD), functools.partial(lambda i, _: (0, i, 0, 0), i))
        for i in range(count)
    ]


def first_phase(blocks, counts, x):
    return pl.pallas_call(
        first_kernel,
        grid=(1,),
        in_specs=[SMEM_SPEC, SMEM_SPEC] + part_specs(3),
        out_specs=[VMEM_SPEC] * 2,
        out_shape=[
            jax.ShapeDtypeStruct((SHARDS, 1, ROWS, HD), bf16),
            jax.ShapeDtypeStruct((NB, 1, BLK), f32),
        ],
        scratch_shapes=[
            pltpu.VMEM((NB + 1, BLK, HD), f32),
            pltpu.VMEM((MAXPAIR, BLK, 2 * BLK), f32),
            pltpu.VMEM((2 * BLK, 2 * BLK), bf16),
            pltpu.VMEM((2 * BLK, 2 * BLK), bf16),
        ],
        compiler_params=pltpu.CompilerParams(vmem_limit_bytes=40 << 20),
        cost_estimate=pl.CostEstimate(
            flops=20_000_000_000, bytes_accessed=6291456, transcendentals=5_000_000
        ),
        name="softmax_and_values",
    )(blocks, counts, x, x, x)


def second_phase(blocks, counts, x, v, lse):
    return pl.pallas_call(
        second_kernel,
        grid=(1,),
        in_specs=[SMEM_SPEC, SMEM_SPEC]
        + part_specs(3)
        + [
            pl.BlockSpec((SHARDS, ROWS, HD), lambda _: (0, 0, 0)),
            pl.BlockSpec((SHARDS, 8, HD), lambda _: (0, ROWS // 8, 0)),
            VMEM_SPEC,
        ],
        out_specs=VMEM_SPEC,
        out_shape=jax.ShapeDtypeStruct((SHARDS, 2, ROWS, HD), bf16),
        scratch_shapes=[
            pltpu.VMEM((NB + 1, BLK, HD), f32),
            pltpu.VMEM((NB, HD, BLK), bf16),
            pltpu.VMEM((NB, 1, BLK), f32),
        ]
        + [pltpu.VMEM((2 * BLK, 2 * BLK), bf16)] * 3,
        compiler_params=pltpu.CompilerParams(vmem_limit_bytes=40 << 20),
        cost_estimate=pl.CostEstimate(
            flops=20_000_000_000, bytes_accessed=9437184, transcendentals=5_000_000
        ),
        name="scores_and_gradients",
    )(blocks, counts, x, x, x, v, v, lse)


def exchange(x):
    return lax.all_to_all(x, "head", split_axis=0, concat_axis=0, tiled=True)


def per_device(queries, key_vectors, values, out_grad, output, key_blocks, block_count):
    parity = (lax.axis_index("head") % 2).astype(jnp.int32).reshape(1)
    blocks = key_blocks[0]
    x = exchange(pack(queries, key_vectors, out_grad))
    v = exchange(pack_values(parity, values, out_grad, output))
    dv, lse = first_phase(blocks, block_count, x)
    (value_grad,) = unpack(exchange(dv))
    query_grad, key_grad = unpack(exchange(second_phase(blocks, block_count, x, v, lse)))
    return query_grad, key_grad, value_grad


def solution(mesh):
    token = P(("dp", "head"), None)
    return jax.shard_map(
        per_device,
        mesh=mesh,
        in_specs=(token,) * 5 + (P(("dp", "head"), None, None), token),
        out_specs=(token,) * 3,
        check_vma=False,
    )
```

```python
import functools

import jax
import jax.numpy as jnp
from jax import lax
from jax.experimental import pallas as pl
from jax.experimental.pallas import tpu as pltpu
from jax.sharding import PartitionSpec as P

HD = 128
BLK = 128
SHARDS = 32
ROWS = 192
TOKENS = SHARDS * ROWS
NB = TOKENS // BLK
KMAX = 12
MAXPAIR = KMAX // 2
COLS = 4
GROUP = 2
SCALE = HD**-0.5
EXP2_SCALE = SCALE * 1.4426950408889634
NEG = -1e30
f32 = jnp.float32
bf16 = jnp.bfloat16

VMEM_SPEC = pl.BlockSpec(memory_space=pltpu.VMEM)
SMEM_SPEC = pl.BlockSpec(memory_space=pltpu.SMEM)


def dot(a, b):
    return lax.dot_general(a, b, (((1,), (0,)), ((), ())), preferred_element_type=f32)


def rows(ref, i):
    return ref[pl.ds(pl.multiple_of(i * BLK, BLK), BLK), :]


def wide(a, b):
    return jnp.concatenate([a, b], axis=1)


def diagonal(ref, x):
    ref[0:BLK, 0:BLK] = x
    ref[BLK : 2 * BLK, BLK : 2 * BLK] = x


def pack_kernel(q_ref, k_ref, g_ref, x_ref):
    for c in range(COLS):
        for i, ref in enumerate((q_ref, k_ref, g_ref)):
            x_ref[c, i] = ref[:, c * HD : (c + 1) * HD]


def pack(q, k, g):
    block = pl.BlockSpec((ROWS, COLS * HD), lambda h: (0, h))
    return pl.pallas_call(
        pack_kernel,
        grid=(SHARDS // COLS,),
        in_specs=[block] * 3,
        out_specs=pl.BlockSpec((COLS, 3, ROWS, HD), lambda h: (h, 0, 0, 0)),
        out_shape=jax.ShapeDtypeStruct((SHARDS, 3, ROWS, HD), bf16),
        cost_estimate=pl.CostEstimate(flops=0, bytes_accessed=9437184, transcendentals=0),
        name="pack_qkg",
    )(q, k, g)


def pack_values_kernel(parity_ref, v_ref, g_ref, o_ref, x_ref):
    odd = parity_ref[0] == 1
    gap = jnp.zeros((64, HD), f32)
    ones = jnp.ones((8, HD), bf16)
    sub = lax.broadcasted_iota(jnp.int32, (8, HD), 0)
    contract = (((1,), (1,)), ((), ()))
    for c in range(COLS):
        cols = slice(c * HD, (c + 1) * HD)
        x_ref[c, 0:ROWS] = v_ref[:, cols]
        prod = g_ref[:, cols].astype(f32) * o_ref[:, cols].astype(f32)
        prod = jnp.where(
            odd, jnp.concatenate([gap, prod], axis=0), jnp.concatenate([prod, gap], axis=0)
        )
        high = prod.astype(bf16)
        low = (prod - high.astype(f32)).astype(bf16)
        terms = lax.dot_general(ones, high, contract, preferred_element_type=f32)
        terms += lax.dot_general(ones, low, contract, preferred_element_type=f32)
        out = jnp.zeros((8, HD), f32)
        rest = terms
        for part in range(3):
            piece = rest.astype(bf16).astype(f32)
            rest = rest - piece
            out = jnp.where(sub == 2 * part, piece[:, :HD], out)
            out = jnp.where(sub == 2 * part + 1, piece[:, HD:], out)
        x_ref[c, ROWS : ROWS + 8] = out.astype(bf16)


def pack_values(parity, v, g, o):
    block = pl.BlockSpec((ROWS, COLS * HD), lambda h: (0, h))
    return pl.pallas_call(
        pack_values_kernel,
        grid=(SHARDS // COLS,),
        in_specs=[SMEM_SPEC] + [block] * 3,
        out_specs=pl.BlockSpec((COLS, ROWS + 8, HD), lambda h: (h, 0, 0)),
        out_shape=jax.ShapeDtypeStruct((SHARDS, ROWS + 8, HD), bf16),
        cost_estimate=pl.CostEstimate(flops=0, bytes_accessed=6291456, transcendentals=0),
        name="pack_v",
    )(parity, v, g, o)


def unpack_kernel(*refs):
    x_ref, outs = refs[0], refs[1:]
    for c in range(COLS):
        for i, ref in enumerate(outs):
            ref[:, c * HD : (c + 1) * HD] = x_ref[c, i]


def unpack(x):
    count = x.shape[1]
    return pl.pallas_call(
        unpack_kernel,
        grid=(SHARDS // COLS,),
        in_specs=[pl.BlockSpec((COLS, count, ROWS, HD), lambda h: (h, 0, 0, 0))],
        out_specs=[pl.BlockSpec((ROWS, COLS * HD), lambda h: (0, h))] * count,
        out_shape=[jax.ShapeDtypeStruct((ROWS, SHARDS * HD), bf16)] * count,
        cost_estimate=pl.CostEstimate(
            flops=0, bytes_accessed=count * 3145728, transcendentals=0
        ),
        compiler_params=pltpu.CompilerParams(vmem_limit_bytes=16 << 20),
        name="unpack",
    )(x)


def store_block(ref, part, block, value):
    for half in range(2):
        piece = 2 * block + half
        shard = piece // 3
        start = pl.multiple_of((piece - 3 * shard) * 64, 64)
        ref[shard, part, pl.ds(start, 64), :] = value[64 * half : 64 * half + 64]


def live_lanes(n, p):
    lane = lax.broadcasted_iota(jnp.int32, (1, 2 * BLK), 1)
    return lane < BLK * (n - 2 * p)


def targets(blocks, a, n, pairs):
    return [jnp.where(s < n, blocks[a, s], NB) for s in range(2 * pairs)]


def gather(ref, blocks, a, pairs):
    return jnp.concatenate(
        [
            wide(rows(ref, blocks[a, 2 * p]), rows(ref, blocks[a, 2 * p + 1]))
            for p in range(pairs)
        ],
        axis=0,
    )


def masked(j, p, pairs):
    return p > 0 and (j < GROUP - 1 or p == pairs - 1)


def add_pairs(acc, where, x, pairs):
    for p in range(pairs):
        piece = x[BLK * p : BLK * (p + 1)]
        b0 = acc[where[2 * p]] + piece[:, :BLK]
        b1 = acc[where[2 * p + 1]] + piece[:, BLK:]
        acc[where[2 * p]] = b0
        acc[where[2 * p + 1]] = b1


def group_loop(order, counts, prepare, work):
    groups = NB // GROUP
    for j in range(GROUP):
        prepare(0, j, order[0, j])

    def body(i, carry):
        slot = i % 2
        ids = [order[0, GROUP * i + j] for j in range(GROUP)]
        ns = [counts[0, a] for a in ids]
        ahead = [order[0, GROUP * jnp.minimum(i + 1, groups - 1) + j] for j in range(GROUP)]

        def run(pairs):
            for j in range(GROUP):
                prepare(1 - slot, j, ahead[j])
            work(slot, ids, ns, pairs)

        for pairs in range(1, MAXPAIR + 1):
            pl.when((ns[-1] + 1) // 2 == pairs)(functools.partial(run, pairs))
        return carry

    lax.fori_loop(0, groups, body, 0)


def first_kernel(order, blocks, counts, q_ref, k_ref, g_ref, dv_ref, lse_ref, acc, st, wq, wg):
    q = q_ref.reshape(TOKENS, HD)
    k = k_ref.reshape(TOKENS, HD)
    g = g_ref.reshape(TOKENS, HD)
    acc[...] = jnp.zeros_like(acc)
    wq[...] = jnp.zeros_like(wq)
    wg[...] = jnp.zeros_like(wg)

    def prepare(slot, j, a):
        diagonal(wq.at[slot, j], rows(q, a).T)
        diagonal(wg.at[slot, j], rows(g, a))

    def work(slot, ids, ns, pairs):
        tops = []
        for j in range(GROUP):
            s = dot(gather(k, blocks, ids[j], pairs), wq[slot, j])
            top = None
            for p in range(pairs):
                piece = s[BLK * p : BLK * (p + 1)]
                if masked(j, p, pairs):
                    piece = jnp.where(live_lanes(ns[j], p), piece, NEG)
                st[j, p] = piece
                here = jnp.max(piece, axis=0, keepdims=True)
                top = here if top is None else jnp.maximum(top, here)
            tops.append(jnp.maximum(top[:, :BLK], top[:, BLK:]) * EXP2_SCALE)
        inverses = []
        for j in range(GROUP):
            top2 = wide(tops[j], tops[j])
            total = None
            for p in range(pairs):
                e = jnp.exp2(st[j, p] * EXP2_SCALE - top2)
                st[j, p] = e
                here = jnp.sum(e, axis=0, keepdims=True)
                total = here if total is None else total + here
            total = total[:, :BLK] + total[:, BLK:]
            lse_ref[ids[j]] = tops[j] + jnp.log2(total)
            inverse = 1.0 / total
            inverses.append(wide(inverse, inverse))
        for j in range(GROUP):
            probs = jnp.concatenate(
                [(st[j, p] * inverses[j]).astype(bf16) for p in range(pairs)], axis=0
            )
            dv = dot(probs, wg[slot, j])
            add_pairs(acc, targets(blocks, ids[j], ns[j], pairs), dv, pairs)

    group_loop(order, counts, prepare, work)

    def finish(b, carry):
        store_block(dv_ref, 0, b, acc[b].astype(bf16))
        return carry

    lax.fori_loop(0, NB, finish, 0, unroll=4)


def second_kernel(
    order, blocks, counts, q_ref, k_ref, g_ref, v_ref, t_ref, lse_ref, out_ref,
    acc, kt, terms, ds_ref, wq, wg, wn,
):
    q = q_ref.reshape(TOKENS, HD)
    k = k_ref.reshape(TOKENS, HD)
    g = g_ref.reshape(TOKENS, HD)
    v = v_ref.reshape(TOKENS, HD)
    acc[...] = jnp.zeros_like(acc)
    wq[...] = jnp.zeros_like(wq)
    wg[...] = jnp.zeros_like(wg)
    wn[...] = jnp.zeros_like(wn)

    def row_terms(t, carry):
        a = t_ref[2 * t].astype(f32)
        b = t_ref[2 * t + 1].astype(f32)
        a0 = a[0:1] + a[2:3] + a[4:5]
        a1 = a[1:2] + a[3:4] + a[5:6]
        b0 = b[0:1] + b[2:3] + b[4:5]
        b1 = b[1:2] + b[3:4] + b[5:6]
        terms[3 * t] = a0
        terms[3 * t + 1] = a1 + b0
        terms[3 * t + 2] = b1
        for r in range(3):
            kt[3 * t + r] = rows(k, 3 * t + r).T
        return carry

    lax.fori_loop(0, NB // 3, row_terms, 0, unroll=2)

    def prepare(slot, j, a):
        qb = rows(q, a)
        diagonal(wq.at[slot, j], qb.T)
        diagonal(wn.at[slot, j], qb)
        diagonal(wg.at[slot, j], rows(g, a).T)

    def work(slot, ids, ns, pairs):
        for j in range(GROUP):
            a = ids[j]
            s = dot(gather(k, blocks, a, pairs), wq[slot, j])
            dp = dot(gather(v, blocks, a, pairs), wg[slot, j])
            lse = wide(lse_ref[a], lse_ref[a])
            term = wide(terms[a], terms[a])
            for p in range(pairs):
                piece = slice(BLK * p, BLK * (p + 1))
                probs = jnp.exp2(s[piece] * EXP2_SCALE - lse)
                if masked(j, p, pairs):
                    probs = jnp.where(live_lanes(ns[j], p), probs, 0.0)
                ds = (probs * (dp[piece] - term)).astype(bf16)
                ds_ref[j, 2 * p] = ds[:, :BLK]
                ds_ref[j, 2 * p + 1] = ds[:, BLK:]
        for j in range(GROUP):
            a = ids[j]
            ds = jnp.concatenate(
                [wide(ds_ref[j, 2 * p], ds_ref[j, 2 * p + 1]) for p in range(pairs)], axis=0
            )
            dk = dot(ds, wn[slot, j])
            add_pairs(acc, targets(blocks, a, ns[j], pairs), dk, pairs)
            keys = jnp.concatenate([kt[blocks[a, s]] for s in range(2 * pairs)], axis=1)
            dq = dot(keys, jnp.concatenate([ds_ref[j, s] for s in range(2 * pairs)], axis=0))
            store_block(out_ref, 0, a, (dq.T * SCALE).astype(bf16))

    group_loop(order, counts, prepare, work)

    def finish(b, carry):
        store_block(out_ref, 1, b, (acc[b] * SCALE).astype(bf16))
        return carry

    lax.fori_loop(0, NB, finish, 0, unroll=4)


def part_specs(count):
    return [
        pl.BlockSpec((SHARDS, None, ROWS, HD), functools.partial(lambda i, _: (0, i, 0, 0), i))
        for i in range(count)
    ]


def first_phase(order, blocks, counts, x):
    return pl.pallas_call(
        first_kernel,
        grid=(1,),
        in_specs=[SMEM_SPEC] * 3 + part_specs(3),
        out_specs=[VMEM_SPEC] * 2,
        out_shape=[
            jax.ShapeDtypeStruct((SHARDS, 1, ROWS, HD), bf16),
            jax.ShapeDtypeStruct((NB, 1, BLK), f32),
        ],
        scratch_shapes=[
            pltpu.VMEM((NB + 1, BLK, HD), f32),
            pltpu.VMEM((GROUP, MAXPAIR, BLK, 2 * BLK), f32),
            pltpu.VMEM((2, GROUP, 2 * BLK, 2 * BLK), bf16),
            pltpu.VMEM((2, GROUP, 2 * BLK, 2 * BLK), bf16),
        ],
        compiler_params=pltpu.CompilerParams(vmem_limit_bytes=40 << 20),
        cost_estimate=pl.CostEstimate(
            flops=20_000_000_000, bytes_accessed=6291456, transcendentals=5_000_000
        ),
        name="softmax_and_values",
    )(order, blocks, counts, x, x, x)


def second_phase(order, blocks, counts, x, v, lse):
    return pl.pallas_call(
        second_kernel,
        grid=(1,),
        in_specs=[SMEM_SPEC] * 3
        + part_specs(3)
        + [
            pl.BlockSpec((SHARDS, ROWS, HD), lambda _: (0, 0, 0)),
            pl.BlockSpec((SHARDS, 8, HD), lambda _: (0, ROWS // 8, 0)),
            VMEM_SPEC,
        ],
        out_specs=VMEM_SPEC,
        out_shape=jax.ShapeDtypeStruct((SHARDS, 2, ROWS, HD), bf16),
        scratch_shapes=[
            pltpu.VMEM((NB + 1, BLK, HD), f32),
            pltpu.VMEM((NB, HD, BLK), bf16),
            pltpu.VMEM((NB, 1, BLK), f32),
            pltpu.VMEM((GROUP, KMAX, BLK, BLK), bf16),
        ]
        + [pltpu.VMEM((2, GROUP, 2 * BLK, 2 * BLK), bf16)] * 3,
        compiler_params=pltpu.CompilerParams(vmem_limit_bytes=40 << 20),
        cost_estimate=pl.CostEstimate(
            flops=20_000_000_000, bytes_accessed=9437184, transcendentals=5_000_000
        ),
        name="scores_and_gradients",
    )(order, blocks, counts, x, x, x, v, v, lse)


def exchange(x):
    return lax.all_to_all(x, "head", split_axis=0, concat_axis=0, tiled=True)


def by_count(counts):
    n = counts[0]
    ids = jnp.arange(NB, dtype=jnp.int32)
    before = (n[None, :] < n[:, None]) | ((n[None, :] == n[:, None]) & (ids[None, :] < ids[:, None]))
    rank = jnp.sum(before.astype(jnp.int32), axis=1)
    return jnp.sum(jnp.where(rank[None, :] == ids[:, None], ids[None, :], 0), axis=1).reshape(1, NB)


def per_device(queries, key_vectors, values, out_grad, output, key_blocks, block_count):
    parity = (lax.axis_index("head") % 2).astype(jnp.int32).reshape(1)
    blocks = key_blocks[0]
    order = by_count(block_count)
    x = exchange(pack(queries, key_vectors, out_grad))
    v = exchange(pack_values(parity, values, out_grad, output))
    dv, lse = first_phase(order, blocks, block_count, x)
    (value_grad,) = unpack(exchange(dv))
    query_grad, key_grad = unpack(exchange(second_phase(order, blocks, block_count, x, v, lse)))
    return query_grad, key_grad, value_grad


def solution(mesh):
    token = P(("dp", "head"), None)
    return jax.shard_map(
        per_device,
        mesh=mesh,
        in_specs=(token,) * 5 + (P(("dp", "head"), None, None), token),
        out_specs=(token,) * 3,
        check_vma=False,
    )
```

```python
import functools

import jax
import jax.numpy as jnp
from jax import lax
from jax.experimental import pallas as pl
from jax.experimental.pallas import tpu as pltpu
from jax.sharding import PartitionSpec as P

HD = 128
BLK = 128
SHARDS = 32
ROWS = 192
TERMS = 16
TOKENS = SHARDS * ROWS
NB = TOKENS // BLK
KMAX = 12
COLS = 4
WIDE = 8
STEPS = SHARDS // WIDE
OUT_STEPS = 8
GROUP = 4
STEP = 2
SCALE = HD**-0.5
EXP2_SCALE = SCALE * 1.4426950408889634
NEG = -1e30
f32 = jnp.float32
bf16 = jnp.bfloat16

VMEM_SPEC = pl.BlockSpec(memory_space=pltpu.VMEM)
ANY_SPEC = pl.BlockSpec(memory_space=pl.ANY)
HBM_SPEC = ANY_SPEC
SMEM_SPEC = pl.BlockSpec(memory_space=pltpu.SMEM)


def dot(a, b):
    return lax.dot_general(a, b, (((1,), (0,)), ((), ())), preferred_element_type=f32)


def rows(ref, i):
    return ref[pl.ds(pl.multiple_of(i * BLK, BLK), BLK), :]


def wide(a, b):
    return jnp.concatenate([a, b], axis=1)


def pack_kernel(q_ref, k_ref, g_ref, out_ref, src, dst, src_sem, dst_sem):
    parts = (q_ref, k_ref, g_ref)

    def read(c, i):
        return pltpu.make_async_copy(
            parts[i].at[:, c * WIDE * HD : (c + 1) * WIDE * HD], src.at[c, i], src_sem.at[c, i]
        )

    def write(c):
        heads = pl.ds(c * WIDE, WIDE)
        return pltpu.make_async_copy(dst.at[heads], out_ref.at[heads], dst_sem.at[c])

    for c in range(STEPS):
        for i in range(3):
            read(c, i).start()
    for c in range(STEPS):
        for i in range(3):
            read(c, i).wait()
            for j in range(WIDE):
                dst[c * WIDE + j, i] = src[c, i, :, j * HD : (j + 1) * HD]
        write(c).start()
    for c in range(STEPS):
        write(c).wait()


def pack(q, k, g):
    return pl.pallas_call(
        pack_kernel,
        in_specs=[ANY_SPEC] * 3,
        out_specs=HBM_SPEC,
        out_shape=jax.ShapeDtypeStruct((SHARDS, 3, ROWS, HD), bf16),
        scratch_shapes=[
            pltpu.VMEM((STEPS, 3, ROWS, WIDE * HD), bf16),
            pltpu.VMEM((SHARDS, 3, ROWS, HD), bf16),
            pltpu.SemaphoreType.DMA((STEPS, 3)),
            pltpu.SemaphoreType.DMA((STEPS,)),
        ],
        compiler_params=pltpu.CompilerParams(vmem_limit_bytes=60 << 20),
        cost_estimate=pl.CostEstimate(flops=0, bytes_accessed=9437184, transcendentals=0),
        name="pack_qkg",
    )(q, k, g)


def pack_values_kernel(parity_ref, v_ref, g_ref, o_ref, x_ref):
    odd = parity_ref[0] == 1
    gap = jnp.zeros((64, HD), f32)
    ones = jnp.ones((8, HD), bf16)
    sub = lax.broadcasted_iota(jnp.int32, (8, HD), 0)
    contract = (((1,), (1,)), ((), ()))
    for c in range(COLS):
        cols = slice(c * HD, (c + 1) * HD)
        x_ref[c, 0:ROWS] = v_ref[:, cols]
        prod = g_ref[:, cols].astype(f32) * o_ref[:, cols].astype(f32)
        prod = jnp.where(
            odd, jnp.concatenate([gap, prod], axis=0), jnp.concatenate([prod, gap], axis=0)
        )
        high = prod.astype(bf16)
        low = (prod - high.astype(f32)).astype(bf16)
        terms = lax.dot_general(ones, high, contract, preferred_element_type=f32)
        terms += lax.dot_general(ones, low, contract, preferred_element_type=f32)
        out = jnp.zeros((8, HD), f32)
        rest = terms
        for part in range(3):
            piece = rest.astype(bf16).astype(f32)
            rest = rest - piece
            out = jnp.where(sub == 2 * part, piece[:, :HD], out)
            out = jnp.where(sub == 2 * part + 1, piece[:, HD:], out)
        x_ref[c, ROWS : ROWS + TERMS] = jnp.concatenate([out, jnp.zeros_like(out)], axis=0).astype(bf16)


def pack_values(parity, v, g, o):
    block = pl.BlockSpec((ROWS, COLS * HD), lambda h: (0, h))
    return pl.pallas_call(
        pack_values_kernel,
        grid=(SHARDS // COLS,),
        in_specs=[SMEM_SPEC] + [block] * 3,
        out_specs=pl.BlockSpec((COLS, ROWS + TERMS, HD), lambda h: (h, 0, 0)),
        out_shape=jax.ShapeDtypeStruct((SHARDS, ROWS + TERMS, HD), bf16),
        cost_estimate=pl.CostEstimate(flops=0, bytes_accessed=6291456, transcendentals=0),
        name="pack_v",
    )(parity, v, g, o)


def unpack_kernel(count, x_ref, *refs):
    outs, (src, dst, src_sem, dst_sem) = refs[:count], refs[count:]

    def read(c):
        heads = pl.ds(c * WIDE, WIDE)
        return pltpu.make_async_copy(x_ref.at[heads], src.at[heads], src_sem.at[c])

    def write(c, i):
        return pltpu.make_async_copy(
            dst.at[c, i], outs[i].at[:, c * WIDE * HD : (c + 1) * WIDE * HD], dst_sem.at[c, i]
        )

    for c in range(STEPS):
        read(c).start()
    for c in range(STEPS):
        read(c).wait()
        for i in range(count):
            for j in range(WIDE):
                dst[c, i, :, j * HD : (j + 1) * HD] = src[c * WIDE + j, i]
            write(c, i).start()
    for c in range(STEPS):
        for i in range(count):
            write(c, i).wait()


def unpack(x):
    count = x.shape[1]
    return pl.pallas_call(
        functools.partial(unpack_kernel, count),
        in_specs=[ANY_SPEC],
        out_specs=[HBM_SPEC] * count,
        out_shape=[jax.ShapeDtypeStruct((ROWS, SHARDS * HD), bf16)] * count,
        scratch_shapes=[
            pltpu.VMEM((SHARDS, count, ROWS, HD), bf16),
            pltpu.VMEM((STEPS, count, ROWS, WIDE * HD), bf16),
            pltpu.SemaphoreType.DMA((STEPS,)),
            pltpu.SemaphoreType.DMA((STEPS, count)),
        ],
        compiler_params=pltpu.CompilerParams(vmem_limit_bytes=24 << 20),
        cost_estimate=pl.CostEstimate(
            flops=0, bytes_accessed=count * 3145728, transcendentals=0
        ),
        name="unpack",
    )(x)


def store_block(ref, part, block, value):
    for half in range(2):
        piece = 2 * block + half
        shard = piece // 3
        start = pl.multiple_of((piece - 3 * shard) * 64, 64)
        ref[shard, part, pl.ds(start, 64), :] = value[64 * half : 64 * half + 64]


def targets(blocks, a, n, slots):
    return [jnp.where(s < n, blocks[a, s], NB) for s in range(slots)]


def gather(ref, blocks, a, slots):
    return jnp.concatenate([rows(ref, blocks[a, s]) for s in range(slots)], axis=0)


def masked(j, s, slots):
    return s > 1 and (j < GROUP - 1 or s > slots - STEP)


def add_slots(acc, where, x, slots):
    for s in range(0, slots, 2):
        take = range(s, min(s + 2, slots))
        sums = [acc[where[t]] + x[BLK * t : BLK * (t + 1)] for t in take]
        for t, total in zip(take, sums):
            acc[where[t]] = total


def group_loop(order, counts, prepare, work):
    groups = NB // GROUP
    for j in range(GROUP):
        prepare(0, j, order[0, j])

    def body(i, carry):
        slot = i % 2
        ids = [order[0, GROUP * i + j] for j in range(GROUP)]
        ns = [counts[0, a] for a in ids]
        ahead = [order[0, GROUP * jnp.minimum(i + 1, groups - 1) + j] for j in range(GROUP)]

        def run(slots):
            for j in range(GROUP):
                prepare(1 - slot, j, ahead[j])
            work(slot, ids, ns, slots)

        for slots in range(2, KMAX + 1, STEP):
            pl.when((ns[-1] + STEP - 1) // STEP * STEP == slots)(functools.partial(run, slots))
        return carry

    lax.fori_loop(0, groups, body, 0)


def load(x_ref, part, buf, sem):
    copy = pltpu.make_async_copy(x_ref.at[:, part], buf, sem)
    copy.start()
    return copy


def finish(acc, scale, buf, part, out_ref, sems):
    shards = SHARDS // OUT_STEPS
    blocks = NB // OUT_STEPS
    copies = []
    for c in range(OUT_STEPS):

        def cast(b, carry):
            store_block(buf, part, b, (acc[b] * scale).astype(bf16))
            return carry

        lax.fori_loop(c * blocks, (c + 1) * blocks, cast, 0, unroll=True)
        here = pl.ds(c * shards, shards)
        copy = pltpu.make_async_copy(buf.at[here, part], out_ref.at[here, part], sems.at[c])
        copy.start()
        copies.append(copy)
    for copy in copies:
        copy.wait()


def first_kernel(
    order, blocks, counts, x_ref, dv_ref, lse_ref,
    q_buf, k_buf, g_buf, out, acc, st, wq, wg, in_sem, out_sem,
):
    copies = [load(x_ref, i, b, in_sem.at[i]) for i, b in enumerate((q_buf, k_buf, g_buf))]
    q = q_buf.reshape(TOKENS, HD)
    k = k_buf.reshape(TOKENS, HD)
    g = g_buf.reshape(TOKENS, HD)
    acc[...] = jnp.zeros_like(acc)
    for copy in copies:
        copy.wait()

    def prepare(slot, j, a):
        wq[slot, j] = rows(q, a).T
        wg[slot, j] = rows(g, a)

    def work(slot, ids, ns, slots):
        tops = []
        for j in range(GROUP):
            scores = dot(gather(k, blocks, ids[j], slots), wq[slot, j])
            top = None
            for s in range(slots):
                piece = scores[BLK * s : BLK * (s + 1)]
                if masked(j, s, slots):
                    piece = jnp.where(s < ns[j], piece, NEG)
                st[j, s] = piece
                here = jnp.max(piece, axis=0, keepdims=True)
                top = here if top is None else jnp.maximum(top, here)
            tops.append(top * EXP2_SCALE)
        inverses = []
        for j in range(GROUP):
            total = None
            for s in range(slots):
                e = jnp.exp2(st[j, s] * EXP2_SCALE - tops[j])
                st[j, s] = e
                here = jnp.sum(e, axis=0, keepdims=True)
                total = here if total is None else total + here
            lse_ref[ids[j]] = tops[j] + jnp.log2(total)
            inverses.append(1.0 / total)
        for j in range(GROUP):
            probs = jnp.concatenate(
                [(st[j, s] * inverses[j]).astype(bf16) for s in range(slots)], axis=0
            )
            dv = dot(probs, wg[slot, j])
            add_slots(acc, targets(blocks, ids[j], ns[j], slots), dv, slots)

    group_loop(order, counts, prepare, work)

    finish(acc, 1.0, out, 0, dv_ref, out_sem)


def second_kernel(
    order, blocks, counts, x_ref, v_ref, lse_ref, out_ref,
    q_buf, k_buf, g_buf, v_buf, t_ref, out, acc, kt, terms, ds_ref, wq, wg, wn, in_sem, out_sem,
):
    k_copy = load(x_ref, 1, k_buf, in_sem.at[0])
    t_copy = load(v_ref, pl.ds(ROWS, TERMS), t_ref, in_sem.at[1])
    copies = [
        load(x_ref, 0, q_buf, in_sem.at[2]),
        load(x_ref, 2, g_buf, in_sem.at[3]),
        load(v_ref, pl.ds(0, ROWS), v_buf, in_sem.at[4]),
    ]
    q = q_buf.reshape(TOKENS, HD)
    k = k_buf.reshape(TOKENS, HD)
    g = g_buf.reshape(TOKENS, HD)
    v = v_buf.reshape(TOKENS, HD)
    acc[...] = jnp.zeros_like(acc)
    k_copy.wait()
    t_copy.wait()

    def row_terms(t, carry):
        a = t_ref[2 * t].astype(f32)
        b = t_ref[2 * t + 1].astype(f32)
        a0 = a[0:1] + a[2:3] + a[4:5]
        a1 = a[1:2] + a[3:4] + a[5:6]
        b0 = b[0:1] + b[2:3] + b[4:5]
        b1 = b[1:2] + b[3:4] + b[5:6]
        terms[3 * t] = a0
        terms[3 * t + 1] = a1 + b0
        terms[3 * t + 2] = b1
        for r in range(3):
            kt[3 * t + r] = rows(k, 3 * t + r).T
        return carry

    lax.fori_loop(0, NB // 3, row_terms, 0, unroll=4)
    for copy in copies:
        copy.wait()

    def prepare(slot, j, a):
        qb = rows(q, a)
        wq[slot, j] = qb.T
        wn[slot, j] = qb
        wg[slot, j] = rows(g, a).T

    def work(slot, ids, ns, slots):
        for j in range(GROUP):
            a = ids[j]
            scores = dot(gather(k, blocks, a, slots), wq[slot, j])
            dp = dot(gather(v, blocks, a, slots), wg[slot, j])
            lse = lse_ref[a]
            term = terms[a]
            for s in range(slots):
                piece = slice(BLK * s, BLK * (s + 1))
                probs = jnp.exp2(scores[piece] * EXP2_SCALE - lse)
                if masked(j, s, slots):
                    probs = jnp.where(s < ns[j], probs, 0.0)
                ds_ref[j, s] = (probs * (dp[piece] - term)).astype(bf16)
        for j in range(GROUP):
            a = ids[j]
            ds = jnp.concatenate([ds_ref[j, s] for s in range(slots)], axis=0)
            dk = dot(ds, wn[slot, j])
            add_slots(acc, targets(blocks, a, ns[j], slots), dk, slots)
            keys = jnp.concatenate([kt[blocks[a, s]] for s in range(slots)], axis=1)
            dq = dot(keys, jnp.concatenate([ds_ref[j, s] for s in range(slots)], axis=0))
            store_block(out, 0, a, (dq.T * SCALE).astype(bf16))

    group_loop(order, counts, prepare, work)

    dq_copy = pltpu.make_async_copy(out.at[:, 0], out_ref.at[:, 0], out_sem.at[OUT_STEPS])
    dq_copy.start()
    finish(acc, SCALE, out, 1, out_ref, out_sem)
    dq_copy.wait()


def first_phase(order, blocks, counts, x):
    return pl.pallas_call(
        first_kernel,
        in_specs=[SMEM_SPEC] * 3 + [ANY_SPEC],
        out_specs=[HBM_SPEC, VMEM_SPEC],
        out_shape=[
            jax.ShapeDtypeStruct((SHARDS, 1, ROWS, HD), bf16),
            jax.ShapeDtypeStruct((NB, 1, BLK), f32),
        ],
        scratch_shapes=[pltpu.VMEM((SHARDS, ROWS, HD), bf16)] * 3
        + [
            pltpu.VMEM((SHARDS, 1, ROWS, HD), bf16),
            pltpu.VMEM((NB + 1, BLK, HD), f32),
            pltpu.VMEM((GROUP, KMAX, BLK, BLK), f32),
            pltpu.VMEM((2, GROUP, BLK, BLK), bf16),
            pltpu.VMEM((2, GROUP, BLK, BLK), bf16),
            pltpu.SemaphoreType.DMA((3,)),
            pltpu.SemaphoreType.DMA((OUT_STEPS,)),
        ],
        compiler_params=pltpu.CompilerParams(vmem_limit_bytes=60 << 20),
        cost_estimate=pl.CostEstimate(
            flops=20_000_000_000, bytes_accessed=6291456, transcendentals=5_000_000
        ),
        name="softmax_and_values",
    )(order, blocks, counts, x)


def second_phase(order, blocks, counts, x, v, lse):
    return pl.pallas_call(
        second_kernel,
        in_specs=[SMEM_SPEC] * 3 + [ANY_SPEC] * 2 + [VMEM_SPEC],
        out_specs=HBM_SPEC,
        out_shape=jax.ShapeDtypeStruct((SHARDS, 2, ROWS, HD), bf16),
        scratch_shapes=[pltpu.VMEM((SHARDS, ROWS, HD), bf16)] * 4
        + [
            pltpu.VMEM((SHARDS, TERMS, HD), bf16),
            pltpu.VMEM((SHARDS, 2, ROWS, HD), bf16),
            pltpu.VMEM((NB + 1, BLK, HD), f32),
            pltpu.VMEM((NB, HD, BLK), bf16),
            pltpu.VMEM((NB, 1, BLK), f32),
            pltpu.VMEM((GROUP, KMAX, BLK, BLK), bf16),
        ]
        + [pltpu.VMEM((2, GROUP, BLK, BLK), bf16)] * 3
        + [pltpu.SemaphoreType.DMA((5,)), pltpu.SemaphoreType.DMA((OUT_STEPS + 1,))],
        compiler_params=pltpu.CompilerParams(vmem_limit_bytes=48 << 20),
        cost_estimate=pl.CostEstimate(
            flops=20_000_000_000, bytes_accessed=9437184, transcendentals=5_000_000
        ),
        name="scores_and_gradients",
    )(order, blocks, counts, x, v, lse)


def exchange(x):
    return lax.all_to_all(x, "head", split_axis=0, concat_axis=0, tiled=True)


def by_count(counts):
    n = counts[0]
    ids = jnp.arange(NB, dtype=jnp.int32)
    before = (n[None, :] < n[:, None]) | ((n[None, :] == n[:, None]) & (ids[None, :] < ids[:, None]))
    rank = jnp.sum(before.astype(jnp.int32), axis=1)
    return jnp.sum(jnp.where(rank[None, :] == ids[:, None], ids[None, :], 0), axis=1).reshape(1, NB)


def per_device(queries, key_vectors, values, out_grad, output, key_blocks, block_count):
    parity = (lax.axis_index("head") % 2).astype(jnp.int32).reshape(1)
    blocks = key_blocks[0]
    order = by_count(block_count)
    x = exchange(pack(queries, key_vectors, out_grad))
    v = exchange(pack_values(parity, values, out_grad, output))
    dv, lse = first_phase(order, blocks, block_count, x)
    (value_grad,) = unpack(exchange(dv))
    query_grad, key_grad = unpack(exchange(second_phase(order, blocks, block_count, x, v, lse)))
    return query_grad, key_grad, value_grad


def solution(mesh):
    token = P(("dp", "head"), None)
    return jax.shard_map(
        per_device,
        mesh=mesh,
        in_specs=(token,) * 5 + (P(("dp", "head"), None, None), token),
        out_specs=(token,) * 3,
        check_vma=False,
    )
```

```python
import functools

import jax
import jax.numpy as jnp
from jax import lax
from jax.experimental import pallas as pl
from jax.experimental.pallas import tpu as pltpu
from jax.sharding import PartitionSpec as P

HD = 128
BLK = 128
SHARDS = 32
ROWS = 192
TERMS = 16
TOKENS = SHARDS * ROWS
NB = TOKENS // BLK
KMAX = 12
COLS = 4
WIDE = 8
STEPS = SHARDS // WIDE
OUT_STEPS = 8
GROUP = 6
STEP = 2
SCALE = HD**-0.5
EXP2_SCALE = SCALE * 1.4426950408889634
NEG = -1e30
f32 = jnp.float32
bf16 = jnp.bfloat16

VMEM_SPEC = pl.BlockSpec(memory_space=pltpu.VMEM)
ANY_SPEC = pl.BlockSpec(memory_space=pl.ANY)
HBM_SPEC = ANY_SPEC
SMEM_SPEC = pl.BlockSpec(memory_space=pltpu.SMEM)


def dot(a, b):
    return lax.dot_general(a, b, (((1,), (0,)), ((), ())), preferred_element_type=f32)


def rows(ref, i):
    return ref[pl.ds(pl.multiple_of(i * BLK, BLK), BLK), :]


def wide(a, b):
    return jnp.concatenate([a, b], axis=1)


def pack_kernel(q_ref, k_ref, g_ref, out_ref, src, dst, src_sem, dst_sem):
    parts = (q_ref, k_ref, g_ref)

    def read(c, i):
        return pltpu.make_async_copy(
            parts[i].at[:, c * WIDE * HD : (c + 1) * WIDE * HD], src.at[c, i], src_sem.at[c, i]
        )

    def write(c):
        heads = pl.ds(c * WIDE, WIDE)
        return pltpu.make_async_copy(dst.at[heads], out_ref.at[heads], dst_sem.at[c])

    for c in range(STEPS):
        for i in range(3):
            read(c, i).start()
    for c in range(STEPS):
        for i in range(3):
            read(c, i).wait()
            for j in range(WIDE):
                dst[c * WIDE + j, i] = src[c, i, :, j * HD : (j + 1) * HD]
        write(c).start()
    for c in range(STEPS):
        write(c).wait()


def pack(q, k, g):
    return pl.pallas_call(
        pack_kernel,
        in_specs=[ANY_SPEC] * 3,
        out_specs=HBM_SPEC,
        out_shape=pltpu.HBM((SHARDS, 3, ROWS, HD), bf16),
        scratch_shapes=[
            pltpu.VMEM((STEPS, 3, ROWS, WIDE * HD), bf16),
            pltpu.VMEM((SHARDS, 3, ROWS, HD), bf16),
            pltpu.SemaphoreType.DMA((STEPS, 3)),
            pltpu.SemaphoreType.DMA((STEPS,)),
        ],
        compiler_params=pltpu.CompilerParams(vmem_limit_bytes=60 << 20),
        cost_estimate=pl.CostEstimate(flops=0, bytes_accessed=9437184, transcendentals=0),
        name="pack_qkg",
    )(q, k, g)


def pack_values_kernel(parity_ref, v_ref, g_ref, o_ref, x_ref):
    odd = parity_ref[0] == 1
    gap = jnp.zeros((64, HD), f32)
    ones = jnp.ones((8, HD), bf16)
    sub = lax.broadcasted_iota(jnp.int32, (8, HD), 0)
    contract = (((1,), (1,)), ((), ()))
    for c in range(COLS):
        cols = slice(c * HD, (c + 1) * HD)
        x_ref[c, 0:ROWS] = v_ref[:, cols]
        prod = g_ref[:, cols].astype(f32) * o_ref[:, cols].astype(f32)
        prod = jnp.where(
            odd, jnp.concatenate([gap, prod], axis=0), jnp.concatenate([prod, gap], axis=0)
        )
        high = prod.astype(bf16)
        low = (prod - high.astype(f32)).astype(bf16)
        terms = lax.dot_general(ones, high, contract, preferred_element_type=f32)
        terms += lax.dot_general(ones, low, contract, preferred_element_type=f32)
        out = jnp.zeros((8, HD), f32)
        rest = terms
        for part in range(3):
            piece = rest.astype(bf16).astype(f32)
            rest = rest - piece
            out = jnp.where(sub == 2 * part, piece[:, :HD], out)
            out = jnp.where(sub == 2 * part + 1, piece[:, HD:], out)
        x_ref[c, ROWS : ROWS + TERMS] = jnp.concatenate([out, jnp.zeros_like(out)], axis=0).astype(bf16)


def pack_values(parity, v, g, o):
    block = pl.BlockSpec((ROWS, COLS * HD), lambda h: (0, h))
    return pl.pallas_call(
        pack_values_kernel,
        grid=(SHARDS // COLS,),
        in_specs=[SMEM_SPEC] + [block] * 3,
        out_specs=pl.BlockSpec((COLS, ROWS + TERMS, HD), lambda h: (h, 0, 0)),
        out_shape=jax.ShapeDtypeStruct((SHARDS, ROWS + TERMS, HD), bf16),
        cost_estimate=pl.CostEstimate(flops=0, bytes_accessed=6291456, transcendentals=0),
        name="pack_v",
    )(parity, v, g, o)


def unpack_kernel(count, x_ref, *refs):
    outs, (src, dst, src_sem, dst_sem) = refs[:count], refs[count:]

    def read(c):
        heads = pl.ds(c * WIDE, WIDE)
        return pltpu.make_async_copy(x_ref.at[heads], src.at[heads], src_sem.at[c])

    def write(c, i):
        return pltpu.make_async_copy(
            dst.at[c, i], outs[i].at[:, c * WIDE * HD : (c + 1) * WIDE * HD], dst_sem.at[c, i]
        )

    for c in range(STEPS):
        read(c).start()
    for c in range(STEPS):
        read(c).wait()
        for i in range(count):
            for j in range(WIDE):
                dst[c, i, :, j * HD : (j + 1) * HD] = src[c * WIDE + j, i]
            write(c, i).start()
    for c in range(STEPS):
        for i in range(count):
            write(c, i).wait()


def unpack(x):
    count = x.shape[1]
    return pl.pallas_call(
        functools.partial(unpack_kernel, count),
        in_specs=[ANY_SPEC],
        out_specs=[HBM_SPEC] * count,
        out_shape=[jax.ShapeDtypeStruct((ROWS, SHARDS * HD), bf16)] * count,
        scratch_shapes=[
            pltpu.VMEM((SHARDS, count, ROWS, HD), bf16),
            pltpu.VMEM((STEPS, count, ROWS, WIDE * HD), bf16),
            pltpu.SemaphoreType.DMA((STEPS,)),
            pltpu.SemaphoreType.DMA((STEPS, count)),
        ],
        compiler_params=pltpu.CompilerParams(vmem_limit_bytes=24 << 20),
        cost_estimate=pl.CostEstimate(
            flops=0, bytes_accessed=count * 3145728, transcendentals=0
        ),
        name="unpack",
    )(x)


def store_block(ref, part, block, value):
    for half in range(2):
        piece = 2 * block + half
        shard = piece // 3
        start = pl.multiple_of((piece - 3 * shard) * 64, 64)
        ref[shard, part, pl.ds(start, 64), :] = value[64 * half : 64 * half + 64]


def targets(blocks, a, n, slots):
    return [jnp.where(s < n, blocks[a, s], NB) for s in range(slots)]


def gather(ref, blocks, a, slots):
    return jnp.concatenate([rows(ref, blocks[a, s]) for s in range(slots)], axis=0)


def masked(j, s, slots):
    return s > 1 and (j < GROUP - 1 or s > slots - STEP)


def add_slots(acc, where, x, slots):
    for s in range(0, slots, 2):
        take = range(s, min(s + 2, slots))
        sums = [acc[where[t]] + x[BLK * t : BLK * (t + 1)] for t in take]
        for t, total in zip(take, sums):
            acc[where[t]] = total


def group_loop(order, counts, prepare, work):
    groups = NB // GROUP
    for j in range(GROUP):
        prepare(0, j, order[0, j])

    def body(i, carry):
        slot = i % 2
        ids = [order[0, GROUP * i + j] for j in range(GROUP)]
        ns = [counts[0, a] for a in ids]
        ahead = [order[0, GROUP * jnp.minimum(i + 1, groups - 1) + j] for j in range(GROUP)]

        def run(slots):
            for j in range(GROUP):
                prepare(1 - slot, j, ahead[j])
            work(slot, ids, ns, slots)

        for slots in range(2, KMAX + 1, STEP):
            pl.when((ns[-1] + STEP - 1) // STEP * STEP == slots)(functools.partial(run, slots))
        return carry

    lax.fori_loop(0, groups, body, 0)


def load(x_ref, part, buf, sem):
    copy = pltpu.make_async_copy(x_ref.at[:, part], buf, sem)
    copy.start()
    return copy


def finish(acc, scale, buf, part, out_ref, sems):
    shards = SHARDS // OUT_STEPS
    blocks = NB // OUT_STEPS
    copies = []
    for c in range(OUT_STEPS):

        def cast(b, carry):
            store_block(buf, part, b, (acc[b] * scale).astype(bf16))
            return carry

        lax.fori_loop(c * blocks, (c + 1) * blocks, cast, 0, unroll=True)
        here = pl.ds(c * shards, shards)
        copy = pltpu.make_async_copy(buf.at[here, part], out_ref.at[here, part], sems.at[c])
        copy.start()
        copies.append(copy)
    for copy in copies:
        copy.wait()


def in_turn(*stages):
    for t in range(GROUP + len(stages) - 1):
        for d, stage in enumerate(stages):
            if 0 <= t - d < GROUP:
                stage(t - d)


def first_kernel(
    order, blocks, counts, x_ref, dv_ref, lse_ref,
    q_buf, k_buf, g_buf, out, acc, st, wq, in_sem, out_sem,
):
    copies = [load(x_ref, i, b, in_sem.at[i]) for i, b in enumerate((q_buf, k_buf, g_buf))]
    q = q_buf.reshape(TOKENS, HD)
    k = k_buf.reshape(TOKENS, HD)
    g = g_buf.reshape(TOKENS, HD)
    acc[...] = jnp.zeros_like(acc)
    for copy in copies:
        copy.wait()

    def prepare(slot, j, a):
        wq[slot, j] = rows(q, a).T

    def work(slot, ids, ns, slots):
        tops, inverses = {}, {}

        def score(j):
            scores = dot(gather(k, blocks, ids[j], slots), wq[slot, j])
            top = None
            for s in range(slots):
                piece = scores[BLK * s : BLK * (s + 1)]
                if masked(j, s, slots):
                    piece = jnp.where(s < ns[j], piece, NEG)
                st[j, s] = piece
                here = jnp.max(piece, axis=0, keepdims=True)
                top = here if top is None else jnp.maximum(top, here)
            tops[j] = top * EXP2_SCALE

        def weigh(j):
            total = None
            for s in range(slots):
                e = jnp.exp2(st[j, s] * EXP2_SCALE - tops[j])
                st[j, s] = e
                here = jnp.sum(e, axis=0, keepdims=True)
                total = here if total is None else total + here
            lse_ref[ids[j]] = tops[j] + jnp.log2(total)
            inverses[j] = 1.0 / total

        def add(j):
            probs = jnp.concatenate(
                [(st[j, s] * inverses[j]).astype(bf16) for s in range(slots)], axis=0
            )
            dv = dot(probs, rows(g, ids[j]))
            add_slots(acc, targets(blocks, ids[j], ns[j], slots), dv, slots)

        in_turn(score, weigh, add)

    group_loop(order, counts, prepare, work)

    finish(acc, 1.0, out, 0, dv_ref, out_sem)


def second_kernel(
    order, blocks, counts, x_ref, v_ref, lse_ref, out_ref,
    q_buf, k_buf, g_buf, v_buf, t_ref, out, acc, kt, terms, ds_ref, wq, wg, wn, in_sem, out_sem,
):
    k_copy = load(x_ref, 1, k_buf, in_sem.at[0])
    t_copy = load(v_ref, pl.ds(ROWS, TERMS), t_ref, in_sem.at[1])
    copies = [
        load(x_ref, 0, q_buf, in_sem.at[2]),
        load(x_ref, 2, g_buf, in_sem.at[3]),
        load(v_ref, pl.ds(0, ROWS), v_buf, in_sem.at[4]),
    ]
    q = q_buf.reshape(TOKENS, HD)
    k = k_buf.reshape(TOKENS, HD)
    g = g_buf.reshape(TOKENS, HD)
    v = v_buf.reshape(TOKENS, HD)
    acc[...] = jnp.zeros_like(acc)
    k_copy.wait()
    t_copy.wait()

    def row_terms(t, carry):
        a = t_ref[2 * t].astype(f32)
        b = t_ref[2 * t + 1].astype(f32)
        a0 = a[0:1] + a[2:3] + a[4:5]
        a1 = a[1:2] + a[3:4] + a[5:6]
        b0 = b[0:1] + b[2:3] + b[4:5]
        b1 = b[1:2] + b[3:4] + b[5:6]
        terms[3 * t] = a0
        terms[3 * t + 1] = a1 + b0
        terms[3 * t + 2] = b1
        for r in range(3):
            kt[3 * t + r] = rows(k, 3 * t + r).T
        return carry

    lax.fori_loop(0, NB // 3, row_terms, 0, unroll=4)
    for copy in copies:
        copy.wait()

    def prepare(slot, j, a):
        qb = rows(q, a)
        wq[slot, j] = qb.T
        wn[slot, j] = qb
        wg[slot, j] = rows(g, a).T

    def work(slot, ids, ns, slots):
        for j in range(GROUP):
            a = ids[j]
            scores = dot(gather(k, blocks, a, slots), wq[slot, j])
            dp = dot(gather(v, blocks, a, slots), wg[slot, j])
            lse = lse_ref[a]
            term = terms[a]
            for s in range(slots):
                piece = slice(BLK * s, BLK * (s + 1))
                probs = jnp.exp2(scores[piece] * EXP2_SCALE - lse)
                if masked(j, s, slots):
                    probs = jnp.where(s < ns[j], probs, 0.0)
                ds_ref[j, s] = (probs * (dp[piece] - term)).astype(bf16)
        for j in range(GROUP):
            a = ids[j]
            ds = jnp.concatenate([ds_ref[j, s] for s in range(slots)], axis=0)
            dk = dot(ds, wn[slot, j])
            add_slots(acc, targets(blocks, a, ns[j], slots), dk, slots)
            keys = jnp.concatenate([kt[blocks[a, s]] for s in range(slots)], axis=1)
            dq = dot(keys, jnp.concatenate([ds_ref[j, s] for s in range(slots)], axis=0))
            store_block(out, 0, a, (dq.T * SCALE).astype(bf16))

    group_loop(order, counts, prepare, work)

    dq_copy = pltpu.make_async_copy(out.at[:, 0], out_ref.at[:, 0], out_sem.at[OUT_STEPS])
    dq_copy.start()
    finish(acc, SCALE, out, 1, out_ref, out_sem)
    dq_copy.wait()


def first_phase(order, blocks, counts, x):
    return pl.pallas_call(
        first_kernel,
        in_specs=[SMEM_SPEC] * 3 + [ANY_SPEC],
        out_specs=[HBM_SPEC, VMEM_SPEC],
        out_shape=[
            pltpu.HBM((SHARDS, 1, ROWS, HD), bf16),
            jax.ShapeDtypeStruct((NB, 1, BLK), f32),
        ],
        scratch_shapes=[pltpu.VMEM((SHARDS, ROWS, HD), bf16)] * 3
        + [
            pltpu.VMEM((SHARDS, 1, ROWS, HD), bf16),
            pltpu.VMEM((NB + 1, BLK, HD), f32),
            pltpu.VMEM((GROUP, KMAX, BLK, BLK), f32),
            pltpu.VMEM((2, GROUP, BLK, BLK), bf16),
            pltpu.SemaphoreType.DMA((3,)),
            pltpu.SemaphoreType.DMA((OUT_STEPS,)),
        ],
        compiler_params=pltpu.CompilerParams(vmem_limit_bytes=40 << 20),
        cost_estimate=pl.CostEstimate(
            flops=20_000_000_000, bytes_accessed=6291456, transcendentals=5_000_000
        ),
        name="softmax_and_values",
    )(order, blocks, counts, x)


def second_phase(order, blocks, counts, x, v, lse):
    return pl.pallas_call(
        second_kernel,
        in_specs=[SMEM_SPEC] * 3 + [ANY_SPEC] * 2 + [VMEM_SPEC],
        out_specs=HBM_SPEC,
        out_shape=pltpu.HBM((SHARDS, 2, ROWS, HD), bf16),
        scratch_shapes=[pltpu.VMEM((SHARDS, ROWS, HD), bf16)] * 4
        + [
            pltpu.VMEM((SHARDS, TERMS, HD), bf16),
            pltpu.VMEM((SHARDS, 2, ROWS, HD), bf16),
            pltpu.VMEM((NB + 1, BLK, HD), f32),
            pltpu.VMEM((NB, HD, BLK), bf16),
            pltpu.VMEM((NB, 1, BLK), f32),
            pltpu.VMEM((GROUP, KMAX, BLK, BLK), bf16),
        ]
        + [pltpu.VMEM((2, GROUP, BLK, BLK), bf16)] * 3
        + [pltpu.SemaphoreType.DMA((5,)), pltpu.SemaphoreType.DMA((OUT_STEPS + 1,))],
        compiler_params=pltpu.CompilerParams(vmem_limit_bytes=40 << 20),
        cost_estimate=pl.CostEstimate(
            flops=20_000_000_000, bytes_accessed=9437184, transcendentals=5_000_000
        ),
        name="scores_and_gradients",
    )(order, blocks, counts, x, v, lse)


def exchange(x):
    return lax.all_to_all(x, "head", split_axis=0, concat_axis=0, tiled=True)


def by_count(counts):
    n = counts[0]
    ids = jnp.arange(NB, dtype=jnp.int32)
    before = (n[None, :] < n[:, None]) | ((n[None, :] == n[:, None]) & (ids[None, :] < ids[:, None]))
    rank = jnp.sum(before.astype(jnp.int32), axis=1)
    return jnp.sum(jnp.where(rank[None, :] == ids[:, None], ids[None, :], 0), axis=1).reshape(1, NB)


def per_device(queries, key_vectors, values, out_grad, output, key_blocks, block_count):
    parity = (lax.axis_index("head") % 2).astype(jnp.int32).reshape(1)
    blocks = key_blocks[0]
    order = by_count(block_count)
    x = exchange(pack(queries, key_vectors, out_grad))
    v = exchange(pack_values(parity, values, out_grad, output))
    dv, lse = first_phase(order, blocks, block_count, x)
    (value_grad,) = unpack(exchange(dv))
    query_grad, key_grad = unpack(exchange(second_phase(order, blocks, block_count, x, v, lse)))
    return query_grad, key_grad, value_grad


def solution(mesh):
    token = P(("dp", "head"), None)
    return jax.shard_map(
        per_device,
        mesh=mesh,
        in_specs=(token,) * 5 + (P(("dp", "head"), None, None), token),
        out_specs=(token,) * 3,
        check_vma=False,
    )
```

```python
import functools

import jax
import jax.numpy as jnp
from jax import lax
from jax.experimental import pallas as pl
from jax.experimental.pallas import tpu as pltpu
from jax.sharding import PartitionSpec as P

HD = 128
BLK = 128
SHARDS = 32
ROWS = 192
TERMS = 8
TOKENS = SHARDS * ROWS
NB = TOKENS // BLK
KMAX = 12
COLS = 4
WIDE = 8
STEPS = SHARDS // WIDE
OUT_STEPS = 8
GROUP = 6
STEP = 2
SCALE = HD**-0.5
EXP2_SCALE = SCALE * 1.4426950408889634
NEG = -1e30
f32 = jnp.float32
bf16 = jnp.bfloat16

VMEM_SPEC = pl.BlockSpec(memory_space=pltpu.VMEM)
ANY_SPEC = pl.BlockSpec(memory_space=pl.ANY)
HBM_SPEC = ANY_SPEC
SMEM_SPEC = pl.BlockSpec(memory_space=pltpu.SMEM)


def dot(a, b):
    return lax.dot_general(a, b, (((1,), (0,)), ((), ())), preferred_element_type=f32)


def rows(ref, i):
    return ref[pl.ds(pl.multiple_of(i * BLK, BLK), BLK), :]


def wide(a, b):
    return jnp.concatenate([a, b], axis=1)


def pack_kernel(q_ref, k_ref, g_ref, out_ref, src, dst, src_sem, dst_sem):
    parts = (q_ref, k_ref, g_ref)

    def read(c, i):
        return pltpu.make_async_copy(
            parts[i].at[:, c * WIDE * HD : (c + 1) * WIDE * HD], src.at[c, i], src_sem.at[c, i]
        )

    def write(c):
        heads = pl.ds(c * WIDE, WIDE)
        return pltpu.make_async_copy(dst.at[heads], out_ref.at[heads], dst_sem.at[c])

    for c in range(STEPS):
        for i in range(3):
            read(c, i).start()
    for c in range(STEPS):
        for i in range(3):
            read(c, i).wait()
            for j in range(WIDE):
                dst[c * WIDE + j, i] = src[c, i, :, j * HD : (j + 1) * HD]
        write(c).start()
    for c in range(STEPS):
        write(c).wait()


def pack(q, k, g):
    return pl.pallas_call(
        pack_kernel,
        in_specs=[ANY_SPEC] * 3,
        out_specs=HBM_SPEC,
        out_shape=pltpu.HBM((SHARDS, 3, ROWS, HD), bf16),
        scratch_shapes=[
            pltpu.VMEM((STEPS, 3, ROWS, WIDE * HD), bf16),
            pltpu.VMEM((SHARDS, 3, ROWS, HD), bf16),
            pltpu.SemaphoreType.DMA((STEPS, 3)),
            pltpu.SemaphoreType.DMA((STEPS,)),
        ],
        compiler_params=pltpu.CompilerParams(vmem_limit_bytes=60 << 20),
        cost_estimate=pl.CostEstimate(flops=0, bytes_accessed=9437184, transcendentals=0),
        name="pack_qkg",
    )(q, k, g)


def pack_values_kernel(parity_ref, v_ref, g_ref, o_ref, x_ref):
    odd = parity_ref[0] == 1
    gap = jnp.zeros((64, HD), f32)
    ones = jnp.ones((8, HD), bf16)
    sub = lax.broadcasted_iota(jnp.int32, (8, HD), 0)
    contract = (((1,), (1,)), ((), ()))
    for c in range(COLS):
        cols = slice(c * HD, (c + 1) * HD)
        x_ref[c, 0:ROWS] = v_ref[:, cols]
        prod = g_ref[:, cols].astype(f32) * o_ref[:, cols].astype(f32)
        prod = jnp.where(
            odd, jnp.concatenate([gap, prod], axis=0), jnp.concatenate([prod, gap], axis=0)
        )
        high = prod.astype(bf16)
        low = (prod - high.astype(f32)).astype(bf16)
        terms = lax.dot_general(ones, high, contract, preferred_element_type=f32)
        terms += lax.dot_general(ones, low, contract, preferred_element_type=f32)
        out = jnp.zeros((8, HD), f32)
        rest = terms
        for part in range(3):
            piece = rest.astype(bf16).astype(f32)
            rest = rest - piece
            out = jnp.where(sub == 2 * part, piece[:, :HD], out)
            out = jnp.where(sub == 2 * part + 1, piece[:, HD:], out)
        x_ref[c, ROWS : ROWS + TERMS] = out.astype(bf16)


def pack_values(parity, v, g, o):
    block = pl.BlockSpec((ROWS, COLS * HD), lambda h: (0, h))
    return pl.pallas_call(
        pack_values_kernel,
        grid=(SHARDS // COLS,),
        in_specs=[SMEM_SPEC] + [block] * 3,
        out_specs=pl.BlockSpec((COLS, ROWS + TERMS, HD), lambda h: (h, 0, 0)),
        out_shape=jax.ShapeDtypeStruct((SHARDS, ROWS + TERMS, HD), bf16),
        cost_estimate=pl.CostEstimate(flops=0, bytes_accessed=6291456, transcendentals=0),
        name="pack_v",
    )(parity, v, g, o)


def unpack_kernel(count, x_ref, *refs):
    outs, (src, dst, src_sem, dst_sem) = refs[:count], refs[count:]

    def read(c):
        heads = pl.ds(c * WIDE, WIDE)
        return pltpu.make_async_copy(x_ref.at[heads], src.at[heads], src_sem.at[c])

    def write(c, i):
        return pltpu.make_async_copy(
            dst.at[c, i], outs[i].at[:, c * WIDE * HD : (c + 1) * WIDE * HD], dst_sem.at[c, i]
        )

    for c in range(STEPS):
        read(c).start()
    for c in range(STEPS):
        read(c).wait()
        for i in range(count):
            for j in range(WIDE):
                dst[c, i, :, j * HD : (j + 1) * HD] = src[c * WIDE + j, i]
            write(c, i).start()
    for c in range(STEPS):
        for i in range(count):
            write(c, i).wait()


def unpack(x):
    count = x.shape[1]
    return pl.pallas_call(
        functools.partial(unpack_kernel, count),
        in_specs=[ANY_SPEC],
        out_specs=[HBM_SPEC] * count,
        out_shape=[jax.ShapeDtypeStruct((ROWS, SHARDS * HD), bf16)] * count,
        scratch_shapes=[
            pltpu.VMEM((SHARDS, count, ROWS, HD), bf16),
            pltpu.VMEM((STEPS, count, ROWS, WIDE * HD), bf16),
            pltpu.SemaphoreType.DMA((STEPS,)),
            pltpu.SemaphoreType.DMA((STEPS, count)),
        ],
        compiler_params=pltpu.CompilerParams(vmem_limit_bytes=24 << 20),
        cost_estimate=pl.CostEstimate(
            flops=0, bytes_accessed=count * 3145728, transcendentals=0
        ),
        name="unpack",
    )(x)


def store_block(ref, part, block, value):
    for half in range(2):
        piece = 2 * block + half
        shard = piece // 3
        start = pl.multiple_of((piece - 3 * shard) * 64, 64)
        ref[shard, part, pl.ds(start, 64), :] = value[64 * half : 64 * half + 64]


def half_rows(ref, piece):
    shard = (piece * 43) >> 7
    start = pl.multiple_of((piece - 3 * shard) * 64, 64)
    return ref[shard, pl.ds(start, 64), :]


def gather_shards(ref, blocks, a, slots):
    return jnp.concatenate(
        [half_rows(ref, 2 * blocks[a, s] + h) for s in range(slots) for h in range(2)], axis=0
    )


def targets(blocks, a, n, slots):
    return [jnp.where(s < n, blocks[a, s], NB) for s in range(slots)]


def gather(ref, blocks, a, slots):
    return jnp.concatenate([rows(ref, blocks[a, s]) for s in range(slots)], axis=0)


def masked(j, s, slots):
    return s > 1 and (j < GROUP - 1 or s > slots - STEP)


def add_slots(acc, where, x, slots):
    for s in range(0, slots, 2):
        take = range(s, min(s + 2, slots))
        sums = [acc[where[t]] + x[BLK * t : BLK * (t + 1)] for t in take]
        for t, total in zip(take, sums):
            acc[where[t]] = total


def group_loop(order, counts, prepare, work):
    groups = NB // GROUP
    for j in range(GROUP):
        prepare(0, j, order[0, j])

    def body(i, carry):
        slot = i % 2
        ids = [order[0, GROUP * i + j] for j in range(GROUP)]
        ns = [counts[0, a] for a in ids]
        ahead = [order[0, GROUP * jnp.minimum(i + 1, groups - 1) + j] for j in range(GROUP)]

        def run(slots):
            for j in range(GROUP):
                prepare(1 - slot, j, ahead[j])
            work(slot, ids, ns, slots)

        for slots in range(2, KMAX + 1, STEP):
            pl.when((ns[-1] + STEP - 1) // STEP * STEP == slots)(functools.partial(run, slots))
        return carry

    lax.fori_loop(0, groups, body, 0)


def load(x_ref, part, buf, sem):
    copy = pltpu.make_async_copy(x_ref.at[:, part], buf, sem)
    copy.start()
    return copy


def finish(acc, scale, buf, part, out_ref, sems):
    shards = SHARDS // OUT_STEPS
    blocks = NB // OUT_STEPS
    copies = []
    for c in range(OUT_STEPS):

        def cast(b, carry):
            store_block(buf, part, b, (acc[b] * scale).astype(bf16))
            return carry

        lax.fori_loop(c * blocks, (c + 1) * blocks, cast, 0, unroll=True)
        here = pl.ds(c * shards, shards)
        copy = pltpu.make_async_copy(buf.at[here, part], out_ref.at[here, part], sems.at[c])
        copy.start()
        copies.append(copy)
    for copy in copies:
        copy.wait()


def in_turn(*stages):
    for t in range(GROUP + len(stages) - 1):
        for d, stage in enumerate(stages):
            if 0 <= t - d < GROUP:
                stage(t - d)


def first_kernel(
    order, blocks, counts, x_ref, dv_ref, lse_ref,
    q_buf, k_buf, g_buf, out, acc, st, wq, in_sem, out_sem,
):
    copies = [load(x_ref, i, b, in_sem.at[i]) for i, b in enumerate((q_buf, k_buf, g_buf))]
    q = q_buf.reshape(TOKENS, HD)
    k = k_buf.reshape(TOKENS, HD)
    g = g_buf.reshape(TOKENS, HD)
    acc[...] = jnp.zeros_like(acc)
    for copy in copies:
        copy.wait()

    def prepare(slot, j, a):
        wq[slot, j] = rows(q, a).T

    def work(slot, ids, ns, slots):
        tops, inverses = {}, {}

        def score(j):
            scores = dot(gather(k, blocks, ids[j], slots), wq[slot, j])
            top = None
            for s in range(slots):
                piece = scores[BLK * s : BLK * (s + 1)]
                if masked(j, s, slots):
                    piece = jnp.where(s < ns[j], piece, NEG)
                st[j, s] = piece
                here = jnp.max(piece, axis=0, keepdims=True)
                top = here if top is None else jnp.maximum(top, here)
            tops[j] = top * EXP2_SCALE

        def weigh(j):
            total = None
            for s in range(slots):
                e = jnp.exp2(st[j, s] * EXP2_SCALE - tops[j])
                st[j, s] = e
                here = jnp.sum(e, axis=0, keepdims=True)
                total = here if total is None else total + here
            lse_ref[ids[j]] = tops[j] + jnp.log2(total)
            inverses[j] = 1.0 / total

        def add(j):
            probs = jnp.concatenate(
                [(st[j, s] * inverses[j]).astype(bf16) for s in range(slots)], axis=0
            )
            dv = dot(probs, rows(g, ids[j]))
            add_slots(acc, targets(blocks, ids[j], ns[j], slots), dv, slots)

        in_turn(score, weigh, add)

    group_loop(order, counts, prepare, work)

    finish(acc, 1.0, out, 0, dv_ref, out_sem)


def second_kernel(
    order, blocks, counts, x_ref, v_ref, lse_ref, out_ref,
    q_buf, k_buf, g_buf, v_buf, out, acc, kt, terms, ds_ref, wq, wg, wn, in_sem, out_sem,
):
    k_copy = load(x_ref, 1, k_buf, in_sem.at[0])
    v_copy = pltpu.make_async_copy(v_ref, v_buf, in_sem.at[1])
    v_copy.start()
    copies = [
        load(x_ref, 0, q_buf, in_sem.at[2]),
        load(x_ref, 2, g_buf, in_sem.at[3]),
    ]
    q = q_buf.reshape(TOKENS, HD)
    k = k_buf.reshape(TOKENS, HD)
    g = g_buf.reshape(TOKENS, HD)
    acc[...] = jnp.zeros_like(acc)
    k_copy.wait()
    v_copy.wait()

    def row_terms(t, carry):
        a = v_buf[2 * t, ROWS : ROWS + TERMS].astype(f32)
        b = v_buf[2 * t + 1, ROWS : ROWS + TERMS].astype(f32)
        a0 = a[0:1] + a[2:3] + a[4:5]
        a1 = a[1:2] + a[3:4] + a[5:6]
        b0 = b[0:1] + b[2:3] + b[4:5]
        b1 = b[1:2] + b[3:4] + b[5:6]
        terms[3 * t] = a0
        terms[3 * t + 1] = a1 + b0
        terms[3 * t + 2] = b1
        for r in range(3):
            kt[3 * t + r] = rows(k, 3 * t + r).T
        return carry

    lax.fori_loop(0, NB // 3, row_terms, 0, unroll=4)
    for copy in copies:
        copy.wait()

    def prepare(slot, j, a):
        qb = rows(q, a)
        wq[slot, j] = qb.T
        wn[slot, j] = qb
        wg[slot, j] = rows(g, a).T

    def work(slot, ids, ns, slots):
        for j in range(GROUP):
            a = ids[j]
            scores = dot(gather(k, blocks, a, slots), wq[slot, j])
            dp = dot(gather_shards(v_buf, blocks, a, slots), wg[slot, j])
            lse = lse_ref[a]
            term = terms[a]
            for s in range(slots):
                piece = slice(BLK * s, BLK * (s + 1))
                probs = jnp.exp2(scores[piece] * EXP2_SCALE - lse)
                if masked(j, s, slots):
                    probs = jnp.where(s < ns[j], probs, 0.0)
                ds_ref[j, s] = (probs * (dp[piece] - term)).astype(bf16)
        for j in range(GROUP):
            a = ids[j]
            ds = jnp.concatenate([ds_ref[j, s] for s in range(slots)], axis=0)
            dk = dot(ds, wn[slot, j])
            add_slots(acc, targets(blocks, a, ns[j], slots), dk, slots)
            keys = jnp.concatenate([kt[blocks[a, s]] for s in range(slots)], axis=1)
            dq = dot(keys, jnp.concatenate([ds_ref[j, s] for s in range(slots)], axis=0))
            store_block(out, 0, a, (dq.T * SCALE).astype(bf16))

    group_loop(order, counts, prepare, work)

    dq_copy = pltpu.make_async_copy(out.at[:, 0], out_ref.at[:, 0], out_sem.at[OUT_STEPS])
    dq_copy.start()
    finish(acc, SCALE, out, 1, out_ref, out_sem)
    dq_copy.wait()


def first_phase(order, blocks, counts, x):
    return pl.pallas_call(
        first_kernel,
        in_specs=[SMEM_SPEC] * 3 + [ANY_SPEC],
        out_specs=[HBM_SPEC, VMEM_SPEC],
        out_shape=[
            pltpu.HBM((SHARDS, 1, ROWS, HD), bf16),
            jax.ShapeDtypeStruct((NB, 1, BLK), f32),
        ],
        scratch_shapes=[pltpu.VMEM((SHARDS, ROWS, HD), bf16)] * 3
        + [
            pltpu.VMEM((SHARDS, 1, ROWS, HD), bf16),
            pltpu.VMEM((NB + 1, BLK, HD), f32),
            pltpu.VMEM((GROUP, KMAX, BLK, BLK), f32),
            pltpu.VMEM((2, GROUP, BLK, BLK), bf16),
            pltpu.SemaphoreType.DMA((3,)),
            pltpu.SemaphoreType.DMA((OUT_STEPS,)),
        ],
        compiler_params=pltpu.CompilerParams(vmem_limit_bytes=40 << 20),
        cost_estimate=pl.CostEstimate(
            flops=20_000_000_000, bytes_accessed=6291456, transcendentals=5_000_000
        ),
        name="softmax_and_values",
    )(order, blocks, counts, x)


def second_phase(order, blocks, counts, x, v, lse):
    return pl.pallas_call(
        second_kernel,
        in_specs=[SMEM_SPEC] * 3 + [ANY_SPEC] * 2 + [VMEM_SPEC],
        out_specs=HBM_SPEC,
        out_shape=pltpu.HBM((SHARDS, 2, ROWS, HD), bf16),
        scratch_shapes=[pltpu.VMEM((SHARDS, ROWS, HD), bf16)] * 3
        + [
            pltpu.VMEM((SHARDS, ROWS + TERMS, HD), bf16),
            pltpu.VMEM((SHARDS, 2, ROWS, HD), bf16),
            pltpu.VMEM((NB + 1, BLK, HD), f32),
            pltpu.VMEM((NB, HD, BLK), bf16),
            pltpu.VMEM((NB, 1, BLK), f32),
            pltpu.VMEM((GROUP, KMAX, BLK, BLK), bf16),
        ]
        + [pltpu.VMEM((2, GROUP, BLK, BLK), bf16)] * 3
        + [pltpu.SemaphoreType.DMA((4,)), pltpu.SemaphoreType.DMA((OUT_STEPS + 1,))],
        compiler_params=pltpu.CompilerParams(vmem_limit_bytes=40 << 20),
        cost_estimate=pl.CostEstimate(
            flops=20_000_000_000, bytes_accessed=9437184, transcendentals=5_000_000
        ),
        name="scores_and_gradients",
    )(order, blocks, counts, x, v, lse)


def exchange(x):
    return lax.all_to_all(x, "head", split_axis=0, concat_axis=0, tiled=True)


def by_count(counts):
    n = counts[0]
    ids = jnp.arange(NB, dtype=jnp.int32)
    before = (n[None, :] < n[:, None]) | ((n[None, :] == n[:, None]) & (ids[None, :] < ids[:, None]))
    rank = jnp.sum(before.astype(jnp.int32), axis=1)
    return jnp.sum(jnp.where(rank[None, :] == ids[:, None], ids[None, :], 0), axis=1).reshape(1, NB)


def per_device(queries, key_vectors, values, out_grad, output, key_blocks, block_count):
    parity = (lax.axis_index("head") % 2).astype(jnp.int32).reshape(1)
    blocks = key_blocks[0]
    order = by_count(block_count)
    x = exchange(pack(queries, key_vectors, out_grad))
    v = exchange(pack_values(parity, values, out_grad, output))
    dv, lse = first_phase(order, blocks, block_count, x)
    (value_grad,) = unpack(exchange(dv))
    query_grad, key_grad = unpack(exchange(second_phase(order, blocks, block_count, x, v, lse)))
    return query_grad, key_grad, value_grad


def solution(mesh):
    token = P(("dp", "head"), None)
    return jax.shard_map(
        per_device,
        mesh=mesh,
        in_specs=(token,) * 5 + (P(("dp", "head"), None, None), token),
        out_specs=(token,) * 3,
        check_vma=False,
    )
```
